512 devices in a mesh: fam: 8 (over y, core), depth: 64 (over x, z).
Axes of the slice: x: 4, y: 4, z: 16, core: 2. Of those that a mesh axis runs over, the one named last changes fastest.
Arguments:
- embedded_homologs: bfloat16 [1024, 256, 768], P(('fam', 'depth')), parts along dimension 0
- normalizer_scale: float32 [768], replicated, may hold values from 0.5 to 1.5
- probe_projector: bfloat16 [768, 768], P('depth')
- lookup_projector: bfloat16 [768, 768], P('depth')
- content_projector: bfloat16 [768, 768], P('depth'), may hold values from -0.21875 to 0.21875
- final_projector: bfloat16 [768, 768], P('depth'), may hold values from -0.21875 to 0.21875
- live_member_tally: int32 [512], P(('fam', 'depth')), parts along dimension 0, may hold values from 1 to 2, 96 in all
Outputs:
- mixed: bfloat16 [1024, 256, 768], P(('fam', 'depth')), parts along dimension 0
The draws below stay inside these ranges and needn't reach their ends.
There are 8 independent parts, one for each index of `fam`. The reference program is written for one: setup_inputs(seed, part) draws one part's arguments, and reference() takes and returns one part's arrays. A program takes and returns all parts, laid end to end along the dimension named above; an argument that names none is the same for every part. Nothing has to cross between parts.
Inputs may be any that keep to these rules, and one draw needn't show every extreme that they name: Device d's live rows are its first live_member_tally[d] slots; one device of each family has all 2 slots live.
All inputs are finite; a program needn't handle non-finite values.
Results may differ from the reference program's by a relative error of at most 0.009.
Values may be sent and summed in bfloat16 or wider, within the bound.
No kernel may reach another device: no remote copies, remote signals or barrier semaphores. Data moves between devices by JAX's collectives and lax.ppermute only.
A program may use at most 64 MiB of HBM per device.

```python
import math
import jax
import jax.numpy as jnp
import numpy as np
from jax import lax

D = 768
HEADS = 12
HD = 64
L = 256
SLOTS = 2
ROWS = 128
N_DEPTH = 64


def shared_normal(key):
    return jax.random.normal(key, (D, D), jnp.float32)


def draw_probe_projector(key, part):
    base = shared_normal(key)
    return (base / jnp.sqrt(jnp.float32(D))).astype(jnp.bfloat16)


def draw_lookup_projector(key, part):
    key = jax.random.fold_in(key, 6)
    own = jax.random.normal(key, (D, D), jnp.float32)
    mixed_draw = own
    return (mixed_draw / jnp.sqrt(jnp.float32(D))).astype(jnp.bfloat16)


def draw_embedded_homologs(key, part):
    key = jax.random.fold_in(key, 7)
    first_key = jax.random.fold_in(key, 0)
    values = jax.random.normal(first_key, (ROWS, L, D), jnp.float32)
    return values.astype(jnp.bfloat16)


def level_of(own_key, shape, cuts, smallest, largest):
    loudness, own = 1.0, jax.random.fold_in(own_key, 6)
    for position, shards_of in cuts:
        heights = jnp.exp(jax.random.uniform(jax.random.fold_in(own, position), (shards_of,), jnp.float32, smallest / len(cuts), largest / len(cuts)))
        loudness = loudness * jnp.repeat(heights, shape[position] // shards_of).reshape([-1 if axis == position else 1 for axis in range(len(shape))])
    return loudness


def length_profile(number_of, total, most, slope):
    weights = [(1 << 20) // math.isqrt(grade ** slope) + 1 for grade in range(2, number_of + 1)]
    spare, counts = total - most - (number_of - 1), [1] * (number_of - 1)
    while spare > 0:
        movable = [i for i in range(number_of - 1) if counts[i] < most]
        pool, remaining = sum([weights[i] for i in movable]), spare
        for i in movable:
            extra = min(most - counts[i], max(1, remaining * weights[i] // pool), spare)
            counts[i] = counts[i] + extra
            spare = spare - extra
    return np.array([most] + counts)


def ragged(stream_key, amount, total, most, lean):
    if amount == 2:
        one = jax.random.randint(stream_key, (), max(1, total - most), min(most, total - 1) + 1)
        return jnp.stack([one, total - one])
    lengths = jnp.asarray(length_profile(amount, total, most, lean), jnp.int32)
    pairs = (amount - 1) // 2
    source_of, taker = lengths[1:1 + 2 * pairs:2], lengths[2:2 + 2 * pairs:2]
    slack = jnp.minimum(source_of - 1, most - taker)
    passed = jax.random.randint(jax.random.fold_in(stream_key, 1), (pairs,), 0, 1 << 20) % (slack + 1)
    lengths = lengths.at[1:1 + 2 * pairs:2].set(source_of - passed).at[2:2 + 2 * pairs:2].set(taker + passed)
    return lengths[jax.random.permutation(jax.random.fold_in(stream_key, 2), amount)]


def bell_draw(key, shape, deviation, reach, pieces=(), kind=jnp.bfloat16):
    array = deviation * jax.random.normal(key, shape, jnp.float32)
    if pieces:
        array = array * level_of(key, shape, pieces, -0.22, 0.18)
    return jnp.clip(array, -reach, reach).astype(kind)


def setup_inputs(seed: int = 0, part: int = 0) -> dict:
    key_of = jax.random.split(jax.random.key(seed), 8)
    own_keys = jax.random.split(jax.random.fold_in(key_of[7], part), 8)
    embedded_homologs = draw_embedded_homologs(jax.random.fold_in(jax.random.fold_in(key_of[7], part), 71), part)
    normalizer_scale = jnp.clip(1.0 + 0.1 * jax.random.normal(key_of[1], (D,), jnp.float32), 0.5, 1.5)
    probe_projector = draw_probe_projector(jax.random.fold_in(key_of[7], 71), part)
    lookup_projector = draw_lookup_projector(jax.random.fold_in(key_of[7], 71), part)
    content_projector = bell_draw(key_of[4], (D, D), D ** -0.5, 0.21875, ((0, 64),))
    final_projector = bell_draw(key_of[5], (D, D), D ** -0.5, 0.21875, ((0, 64),))
    live_member_tally = ragged(own_keys[6], N_DEPTH, (N_DEPTH * (SLOTS + 1)) // 2, SLOTS, 2).astype(jnp.int32)
    return dict(embedded_homologs=embedded_homologs, normalizer_scale=normalizer_scale, probe_projector=probe_projector, lookup_projector=lookup_projector, content_projector=content_projector, final_projector=final_projector, live_member_tally=live_member_tally)


def reference(embedded_homologs, normalizer_scale, probe_projector, lookup_projector, content_projector, final_projector, live_member_tally):
    homolog_entries = embedded_homologs.shape[0]
    incoming_features = embedded_homologs.astype(jnp.float32)
    mean = lax.optimization_barrier(jnp.mean(incoming_features, axis=-1, keepdims=True))
    var = lax.optimization_barrier(jnp.mean((incoming_features - mean) ** 2, axis=-1, keepdims=True))
    normed = ((incoming_features - mean) / jnp.sqrt(var + 1e-05) * normalizer_scale).astype(jnp.bfloat16)
    flat = normed.reshape(homolog_entries * L, D)
    live = (jnp.arange(SLOTS)[None, :] < live_member_tally[:, None]).reshape(-1).astype(jnp.float32)
    depth = jnp.sum(live_member_tally).astype(jnp.float32)
    query = (jnp.dot(flat, probe_projector, preferred_element_type=jnp.float32).reshape(homolog_entries, L, D) * live[:, None, None]).astype(jnp.bfloat16)
    keys = jnp.dot(flat, lookup_projector, preferred_element_type=jnp.float32).astype(jnp.bfloat16)
    value = jnp.dot(flat, content_projector, preferred_element_type=jnp.float32).astype(jnp.bfloat16)
    query = query.reshape(homolog_entries, L, HEADS, HD).astype(jnp.float32)
    keys = keys.reshape(homolog_entries, L, HEADS, HD).astype(jnp.float32)
    value = value.reshape(homolog_entries, L, HEADS, HD).astype(jnp.float32)
    summed = jnp.einsum('rihe,rjhe->hij', query, keys)
    logits = summed / (math.sqrt(HD) * jnp.sqrt(depth))
    probs = jax.nn.softmax(logits, axis=-1).astype(jnp.bfloat16)
    context = jnp.einsum('hij,rjhe->rihe', probs.astype(jnp.float32), value).astype(jnp.bfloat16)
    mixed = jnp.dot(context.reshape(homolog_entries * L, D), final_projector, preferred_element_type=jnp.float32).reshape(homolog_entries, L, D)
    return (mixed * live[:, None, None]).astype(jnp.bfloat16)
```

```python
import functools
import math

import jax
import jax.numpy as jnp
from jax import lax
from jax.experimental import pallas as pl
from jax.experimental.pallas import tpu as pltpu
from jax.sharding import Mesh, PartitionSpec as P

D = 768
HEADS = 12
HD = 64
L = 256
NY, NC, NX, NZ = 4, 2, 4, 16
ND = NX * NZ
HX = HEADS // NX
WX = HX * HD
ROWS = D // ND
RY = ROWS // NY
BF = jnp.bfloat16
F32 = jnp.float32
VMEM = pl.BlockSpec(memory_space=pltpu.VMEM)
SMEM = pl.BlockSpec(memory_space=pltpu.SMEM)
VLIMIT = 24 * 1024 * 1024


def call(body, out, ins, scratch=(), flops=0, nbytes=1 << 20, name=None):
    return pl.pallas_call(
        body,
        out_shape=out,
        in_specs=ins,
        out_specs=jax.tree.map(lambda _: VMEM, out),
        scratch_shapes=list(scratch),
        compiler_params=pltpu.CompilerParams(vmem_limit_bytes=VLIMIT),
        cost_estimate=pl.CostEstimate(flops=flops, bytes_accessed=nbytes, transcendentals=0),
        name=name,
    )


def norm_body(tally, x_ref, scale_ref, out_ref):
    for r in range(2):
        x = x_ref[r * L : (r + 1) * L, :].astype(F32)
        mean = jnp.sum(x, axis=-1, keepdims=True) * (1.0 / D)
        x = x - mean
        var = jnp.sum(x * x, axis=-1, keepdims=True) * (1.0 / D)
        normed = (x * lax.rsqrt(var + 1e-05) * scale_ref[...]).astype(BF)
        live = (r < tally[0]).astype(BF)
        out_ref[r * L : (r + 1) * L, :] = normed * live


def pack_body(me, tally, q_ref, k_ref, v_ref, o_ref, out_ref, tile):
    y, first = me[1], me[2] == 0

    def rows(ref):
        all_rows = ref[...].astype(F32)
        got = all_rows[:RY]
        for i in range(1, NY):
            got = jnp.where(y == i, all_rows[i * RY : i * RY + RY], got)
        return got

    q, k, v, o = rows(q_ref), rows(k_ref), rows(v_ref), rows(o_ref)
    o = jnp.where(first, o[:, :384], o[:, 384:])
    count = jnp.full((1, 32), tally[0].astype(F32))
    for x in range(NX):
        mine = jnp.concatenate([w[:, WX * x : WX * x + WX] for w in (q, k, v)], axis=1)
        main = jnp.where(first, mine[:, :256], mine[:, 256:512])
        rest = jnp.where(first, mine[:, 512:544], mine[:, 544:576])
        for r in range(RY):
            for c in range(2):
                tile[2 * r + c : 2 * r + c + 1, :] = main[r : r + 1, 128 * c : 128 * c + 128]
            for c in range(3):
                tile[7 + 3 * r + c : 8 + 3 * r + c, :] = o[r : r + 1, 128 * c : 128 * c + 128]
        tile[6:7, :] = jnp.concatenate([rest[r : r + 1] for r in range(RY)] + [count], axis=1)
        made = tile[...].astype(BF)
        for z in range(NZ):
            out_ref[x * NZ + z] = made


def split_body(pieces_ref, early_ref, late_ref, count_ref):
    early = pieces_ref[:, 0:8, :]
    for y in range(NY):
        early_ref[y] = early
    late_ref[...] = pieces_ref[:, 8:16, :].reshape(ND * 8, 128)
    count_ref[...] = jnp.sum(early[:, 6, :].astype(F32), axis=0, keepdims=True)


def take(held, core, y, s):
    return held[core, y, pl.ds(s, ND, stride=8), :]


def in_body(me, own_ref, other_ref, w_ref, held, wide):
    core = me[2]
    held[core] = own_ref[...].astype(F32)
    held[1 - core] = other_ref[...].astype(F32)
    for y in range(NY):
        rest = [take(held, c, y, 6) for c in range(2)]
        for r in range(RY):
            rows = pl.ds(y * RY + r, ND, stride=ROWS)
            for k in range(4):
                wide[k, rows, :] = take(held, k // 2, y, 2 * r + k % 2)
            cut = [part[:, 32 * r : 32 * r + 32] for part in rest]
            wide[4, rows, :] = jnp.concatenate(cut + [jnp.zeros((ND, 64), F32)], axis=1)
    for k in range(5):
        w_ref[:, 128 * k : 128 * k + 128] = wide[k].astype(BF)


def out_body(me, own_a, other_a, own_b, other_b, w_ref, held_a, held_b, wide):
    y0, core = me[1], me[2]
    held_a[core] = own_a[...].astype(F32)
    held_a[1 - core] = other_a[...].astype(F32)
    for g, back in enumerate((0, 1, -1, 2)):
        y = (y0 - back + NY) % NY
        held_b[core, y] = own_b[g].astype(F32)
        held_b[1 - core, y] = other_b[g].astype(F32)
    for y in range(NY):
        for r in range(RY):
            rows = pl.ds(y * RY + r, ND, stride=ROWS)
            for c in range(2):
                for k in range(3):
                    s = 7 + 3 * r + k
                    wide[3 * c + k, rows, :] = take(held_a, c, y, s) if s < 8 else take(held_b, c, y, s - 8)
    for k in range(6):
        w_ref[:, 128 * k : 128 * k + 128] = wide[k].astype(BF)


def side_by_side(array, start):
    return jnp.concatenate([array[:L, start : start + HD], array[L:, start : start + HD]], axis=1)


def logits_body(x0, x1, x2, x3, x4, w_ref, s_ref, v_ref, total):
    project = lambda ref: jnp.dot(ref[...], w_ref[...], preferred_element_type=F32).astype(BF)
    for g in range(4):
        made = project((x0, x1, x2)[g]) if g < 3 else jnp.concatenate([project(x3), project(x4)], axis=0)
        for h in range(HX):
            q = side_by_side(made, h * HD)
            k = side_by_side(made, WX + h * HD)
            v_ref[h, :, 128 * g : 128 * g + 128] = side_by_side(made, 2 * WX + h * HD)
            s = lax.dot_general(q, k, (((1,), (1,)), ((), ())), preferred_element_type=F32)
            if g == 0:
                total[h] = s
            elif g < 3:
                total[h] += s
            else:
                s_ref[:, 16 * h : 16 * h + 16, :] = (total[h] + s).astype(BF).reshape(NZ, 16, L)


def softmax_body(count_ref, s_ref, p_ref):
    depth = count_ref[...][:, 96:97]
    s = s_ref[0].astype(F32)
    for z in range(1, NZ):
        s = s + s_ref[z].astype(F32)
    s = s / (math.sqrt(HD) * jnp.sqrt(depth))
    e = jnp.exp(s - jnp.max(s, axis=-1, keepdims=True))
    p = (e / jnp.sum(e, axis=-1, keepdims=True)).astype(BF)
    for z in range(NZ):
        p_ref[z] = p


def context_body(me, p_ref, v_ref, c_ref):
    x = me[0]
    for h in range(HX):
        p = p_ref[:, 16 * h : 16 * h + 16, :].reshape(L, L)
        made = jnp.dot(p, v_ref[h], preferred_element_type=F32).astype(BF)
        for g, back in enumerate((0, 1, -1, 2)):
            to = (x - back + NX) % NX
            c_ref[to, :, 128 * h : 128 * h + 128] = made[:, 128 * g : 128 * g + 128]


def mixed_body(tally, c_ref, w_ref, out_ref):
    chunks = [c_ref[h // HX, :, 128 * (h % HX) : 128 * (h % HX) + 128] for h in range(HEADS)]
    for r in range(2):
        a = jnp.concatenate([chunk[:, HD * r : HD * r + HD] for chunk in chunks], axis=1)
        made = jnp.dot(a, w_ref[...], preferred_element_type=F32)
        out_ref[r] = (made * (r < tally[0]).astype(F32)).astype(BF)


def struct(shape, dtype=BF):
    return jax.ShapeDtypeStruct(shape, dtype)


def per_device(x, scale, probe, lookup, content, final, tally):
    me = jnp.stack([lax.axis_index("x"), lax.axis_index("y"), lax.axis_index("core")]).astype(jnp.int32)
    shift = lambda a, axis, n, d: lax.ppermute(a, axis, [(i, (i + d) % n) for i in range(n)])
    fence = lambda *a: lax.optimization_barrier(a)

    pieces = call(pack_body, struct((ND, 16, 128)), [SMEM, SMEM] + [VMEM] * 4, [pltpu.VMEM((16, 128), F32)], name="pack")(
        me, tally, probe, lookup, content, final
    )
    normed = call(norm_body, struct((2 * L, D)), [SMEM, VMEM, VMEM], flops=1 << 22, nbytes=1 << 21, name="norm")(
        tally, x.reshape(2 * L, D), scale.reshape(1, D)
    )
    pieces = lax.all_to_all(pieces, ("x", "z"), 0, 0, tiled=True)
    near, far = shift(normed, "x", NX, 1), shift(normed, "x", NX, -1)
    over, under = shift(near[:L], "x", NX, 1), shift(far[L:], "x", NX, -1)

    pieces, over, under = fence(pieces, over, under)
    early, late, count = call(
        split_body,
        (struct((NY, ND, 8, 128)), struct((ND * 8, 128)), struct((1, 128), F32)),
        [VMEM],
        name="split",
    )(pieces)
    own = lax.all_to_all(early, "y", 0, 0, tiled=True)
    other = shift(own, "core", 2, 1)
    own, other = own.reshape(NY, ND * 8, 128), other.reshape(NY, ND * 8, 128)
    held = pltpu.VMEM((2, NY, ND * 8, 128), F32)
    wide = pltpu.VMEM((6, D, 128), F32)
    w_in = call(in_body, struct((D, 640)), [SMEM, VMEM, VMEM], [held, wide], 1 << 20, 1 << 22, name="unpack_in")(
        me, own, other
    )
    s, v = call(
        logits_body,
        (struct((NZ, 16 * HX, L)), struct((HX, L, 8 * HD))),
        [VMEM] * 6,
        [pltpu.VMEM((HX, L, L), F32)],
        flops=3 << 30,
        nbytes=1 << 23,
        name="logits",
    )(normed, near, far, over, under, w_in)

    s, late = fence(s, late)
    lates = [late] + [shift(late, "y", NY, d) for d in (1, -1, 2)]
    s = lax.all_to_all(s, "z", 0, 0, tiled=True)
    s, *lates = fence(s, *lates)
    p = call(softmax_body, struct((NZ, 16 * HX, L)), [VMEM, VMEM], flops=1 << 20, name="softmax")(count, s)
    own_late = jnp.stack(lates)
    p, own_late = fence(p, own_late)
    other_late = shift(own_late, "core", 2, 1)
    p = lax.all_to_all(p, "z", 0, 0, tiled=True)
    p, other_late = fence(p, other_late)
    c = call(context_body, struct((NX, L, 2 * WX)), [SMEM, VMEM, VMEM], flops=1 << 29, name="context")(me, p, v)
    w_out = call(out_body, struct((D, D)), [SMEM] + [VMEM] * 4, [held, held, wide], 1 << 20, 1 << 22, name="unpack_out")(
        me, own, other, own_late, other_late
    )
    c = lax.all_to_all(c, "x", 0, 0, tiled=True)
    return call(mixed_body, struct((2, L, D)), [SMEM, VMEM, VMEM], flops=1 << 30, name="mix")(tally, c, w_out)


def solution(mesh):
    axes = ("y", "core", "x", "z")
    grid = Mesh(mesh.devices.reshape(NY, NC, NX, NZ), axes)
    weight = P(("x", "z"), None)
    return jax.shard_map(
        per_device,
        mesh=grid,
        in_specs=(P(axes, None, None), P(), weight, weight, weight, weight, P(axes)),
        out_specs=P(axes, None, None),
        check_vma=False,
    )
```

```python
import functools
import math

import jax
import jax.numpy as jnp
from jax import lax
from jax.experimental import pallas as pl
from jax.experimental.pallas import tpu as pltpu
from jax.sharding import Mesh, PartitionSpec as P

D = 768
HEADS = 12
HD = 64
L = 256
NY, NC, NX, NZ = 4, 2, 4, 16
ND = NX * NZ
HX = HEADS // NX
WX = HX * HD
ROWS = D // ND
RY = ROWS // NY
BF = jnp.bfloat16
F32 = jnp.float32
VMEM = pl.BlockSpec(memory_space=pltpu.VMEM)
ANY = pl.BlockSpec()
HBM = pl.BlockSpec(memory_space=pltpu.HBM)
SMEM = pl.BlockSpec(memory_space=pltpu.SMEM)
VLIMIT = 24 * 1024 * 1024
VMOST = 60 * 1024 * 1024


def call(body, out, ins, scratch=(), flops=0, nbytes=1 << 20, name=None, outs=None, limit=VLIMIT):
    return pl.pallas_call(
        body,
        out_shape=out,
        in_specs=ins,
        out_specs=outs or jax.tree.map(lambda _: VMEM, out),
        scratch_shapes=list(scratch),
        compiler_params=pltpu.CompilerParams(vmem_limit_bytes=limit),
        cost_estimate=pl.CostEstimate(flops=flops, bytes_accessed=nbytes, transcendentals=0),
        name=name,
    )


def first_body(me, tally, x_hbm, g_hbm, q_hbm, k_hbm, v_hbm, o_hbm, out_ref, normed_ref, x_ref, g_ref, near, tile, sems):
    y, first = me[0] // 128, me[0] // 64 % 2 == 0
    weights = [pltpu.make_async_copy(w, near.at[i], sems.at[i]) for i, w in enumerate((q_hbm, k_hbm, v_hbm, o_hbm))]
    others = [pltpu.make_async_copy(x_hbm, x_ref, sems.at[4]), pltpu.make_async_copy(g_hbm, g_ref, sems.at[5])]
    for copy in weights + others:
        copy.start()
    for copy in weights:
        copy.wait()

    def rows(i):
        all_rows = near[i].astype(F32)
        got = all_rows[:RY]
        for j in range(1, NY):
            got = jnp.where(y == j, all_rows[j * RY : j * RY + RY], got)
        return got

    q, k, v, o = (rows(i) for i in range(4))
    o = jnp.where(first, o[:, :384], o[:, 384:])
    count = jnp.full((1, 32), tally[0].astype(F32))
    for x in range(NX):
        mine = jnp.concatenate([w[:, WX * x : WX * x + WX] for w in (q, k, v)], axis=1)
        main = jnp.where(first, mine[:, :256], mine[:, 256:512])
        rest = jnp.where(first, mine[:, 512:544], mine[:, 544:576])
        for r in range(RY):
            for c in range(2):
                tile[2 * r + c : 2 * r + c + 1, :] = main[r : r + 1, 128 * c : 128 * c + 128]
            for c in range(3):
                tile[7 + 3 * r + c : 8 + 3 * r + c, :] = o[r : r + 1, 128 * c : 128 * c + 128]
        tile[6:7, :] = jnp.concatenate([rest[r : r + 1] for r in range(RY)] + [count], axis=1)
        made = tile[...].astype(BF)
        for z in range(NZ):
            out_ref[x * NZ + z] = made
    for copy in others:
        copy.wait()
    scale = g_ref[...].reshape(1, D)
    for r in range(2):
        x = x_ref[r * L : (r + 1) * L, :].astype(F32)
        mean = jnp.sum(x, axis=-1, keepdims=True) * (1.0 / D)
        x = x - mean
        var = jnp.sum(x * x, axis=-1, keepdims=True) * (1.0 / D)
        normed = (x * lax.rsqrt(var + 1e-05) * scale).astype(BF)
        live = (r < tally[0]).astype(BF)
        normed_ref[r * L : (r + 1) * L, :] = normed * live


def split_body(pieces_ref, early_ref, late_ref, count_ref):
    early = pieces_ref[:, 0:8, :]
    for y in range(NY):
        early_ref[y] = early
    late_ref[...] = pieces_ref[:, 8:16, :].reshape(ND * 8, 128)
    count_ref[...] = jnp.sum(early[:, 6, :].astype(F32), axis=0, keepdims=True)


def take(held, core, y, s):
    return held[core, y, pl.ds(s, ND, stride=8), :]


def in_body(me, own_ref, other_ref, w_ref, held, wide):
    core = me[0] // 64 % 2
    held[core] = own_ref[...].astype(F32)
    held[1 - core] = other_ref[...].astype(F32)
    for y in range(NY):
        rest = [take(held, c, y, 6) for c in range(2)]
        for r in range(RY):
            rows = pl.ds(y * RY + r, ND, stride=ROWS)
            for k in range(4):
                wide[k, rows, :] = take(held, k // 2, y, 2 * r + k % 2)
            cut = [part[:, 32 * r : 32 * r + 32] for part in rest]
            wide[4, rows, :] = jnp.concatenate(cut + [jnp.zeros((ND, 64), F32)], axis=1)
    for k in range(5):
        w_ref[:, 128 * k : 128 * k + 128] = wide[k].astype(BF)


def out_body(me, own_a, other_a, own_b, other_b, w_ref, held_a, held_b, wide):
    y0, core = me[0] // 128, me[0] // 64 % 2
    held_a[core] = own_a[...].astype(F32)
    held_a[1 - core] = other_a[...].astype(F32)
    for g, back in enumerate((0, 1, -1, 2)):
        y = (y0 - back + NY) % NY
        held_b[core, y] = own_b[g].astype(F32)
        held_b[1 - core, y] = other_b[g].astype(F32)
    for y in range(NY):
        for r in range(RY):
            rows = pl.ds(y * RY + r, ND, stride=ROWS)
            for c in range(2):
                for k in range(3):
                    s = 7 + 3 * r + k
                    wide[3 * c + k, rows, :] = take(held_a, c, y, s) if s < 8 else take(held_b, c, y, s - 8)
    for k in range(6):
        w_ref[:, 128 * k : 128 * k + 128] = wide[k].astype(BF)


def side_by_side(array, start):
    return jnp.concatenate([array[:L, start : start + HD], array[L:, start : start + HD]], axis=1)


def logits_body(x0, x1, x2, x3, w_ref, s_ref, v_ref, total):
    for g, x_ref in enumerate((x0, x1, x2, x3)):
        made = jnp.dot(x_ref[...], w_ref[...], preferred_element_type=F32).astype(BF)
        for h in range(HX):
            q = side_by_side(made, h * HD)
            k = side_by_side(made, WX + h * HD)
            v_ref[h, :, 128 * g : 128 * g + 128] = side_by_side(made, 2 * WX + h * HD)
            s = lax.dot_general(q, k, (((1,), (1,)), ((), ())), preferred_element_type=F32)
            if g == 0:
                total[h] = s
            elif g < 3:
                total[h] += s
            else:
                s_ref[:, 16 * h : 16 * h + 16, :] = (total[h] + s).astype(BF).reshape(NZ, 16, L)


def softmax_body(count_ref, s_ref, p_ref):
    depth = count_ref[...][:, 96:97]
    s = s_ref[0].astype(F32)
    for z in range(1, NZ):
        s = s + s_ref[z].astype(F32)
    s = s / (math.sqrt(HD) * jnp.sqrt(depth))
    e = jnp.exp(s - jnp.max(s, axis=-1, keepdims=True))
    p = (e / jnp.sum(e, axis=-1, keepdims=True)).astype(BF)
    for z in range(NZ):
        p_ref[z] = p


def context_body(me, p_ref, v_ref, c_ref):
    x = me[0] // 16 % 4
    for h in range(HX):
        p = p_ref[:, 16 * h : 16 * h + 16, :].reshape(L, L)
        made = jnp.dot(p, v_ref[h], preferred_element_type=F32).astype(BF)
        for g, back in enumerate((0, 1, -1, 2)):
            to = (x - back + NX) % NX
            c_ref[to, :, 128 * h : 128 * h + 128] = made[:, 128 * g : 128 * g + 128]


def mixed_body(tally, c_ref, w_ref, out_ref):
    chunks = [c_ref[h // HX, :, 128 * (h % HX) : 128 * (h % HX) + 128] for h in range(HEADS)]
    for r in range(2):
        a = jnp.concatenate([chunk[:, HD * r : HD * r + HD] for chunk in chunks], axis=1)
        made = jnp.dot(a, w_ref[...], preferred_element_type=F32)
        out_ref[r] = (made * (r < tally[0]).astype(F32)).astype(BF)


def struct(shape, dtype=BF):
    return jax.ShapeDtypeStruct(shape, dtype)


def per_device(x, scale, probe, lookup, content, final, tally):
    me = lax.axis_index(("y", "core", "x", "z")).astype(jnp.int32).reshape(1)
    shift = lambda a, axis, n, d: lax.ppermute(a, axis, [(i, (i + d) % n) for i in range(n)])
    fence = lambda *a: lax.optimization_barrier(a)

    pieces, normed = call(
        first_body,
        (struct((ND, 16, 128)), struct((2 * L, D))),
        [SMEM, SMEM] + [HBM] * 6,
        [
            pltpu.VMEM((2 * L, D), BF),
            pltpu.VMEM((D,), F32),
            pltpu.VMEM((4, ROWS, D), BF),
            pltpu.VMEM((16, 128), F32),
            pltpu.SemaphoreType.DMA((6,)),
        ],
        name="first",
        outs=(ANY, ANY),
        limit=VMOST,
    )(me, tally, x.reshape(2 * L, D), scale, probe, lookup, content, final)
    pieces = lax.all_to_all(pieces, ("x", "z"), 0, 0, tiled=True)
    near, far = shift(normed, "x", NX, 1), shift(normed, "x", NX, -1)
    across = shift(near, "x", NX, 1)

    early, late, count = call(
        split_body,
        (struct((NY, ND, 8, 128)), struct((ND * 8, 128)), struct((1, 128), F32)),
        [VMEM],
        name="split",
    )(pieces)
    own = lax.all_to_all(early, "y", 0, 0, tiled=True)
    own, far, across = fence(own, far, across)
    other = shift(own, "core", 2, 1)
    own, other = own.reshape(NY, ND * 8, 128), other.reshape(NY, ND * 8, 128)
    held = pltpu.VMEM((2, NY, ND * 8, 128), F32)
    wide = pltpu.VMEM((6, D, 128), F32)
    w_in = call(in_body, struct((D, 640)), [SMEM, VMEM, VMEM], [held, wide], 1 << 20, 1 << 22, name="unpack_in")(
        me, own, other
    )
    s, v = call(
        logits_body,
        (struct((NZ, 16 * HX, L)), struct((HX, L, 8 * HD))),
        [VMEM] * 5,
        [pltpu.VMEM((HX, L, L), F32)],
        flops=3 << 30,
        nbytes=1 << 23,
        name="logits",
    )(normed, near, far, across, w_in)

    s, late = fence(s, late)
    lates = [late] + [shift(late, "y", NY, d) for d in (1, -1, 2)]
    s = lax.all_to_all(s, "z", 0, 0, tiled=True)
    s, *lates = fence(s, *lates)
    p = call(softmax_body, struct((NZ, 16 * HX, L)), [VMEM, VMEM], flops=1 << 20, name="softmax")(count, s)
    own_late = jnp.stack(lates)
    p, own_late = fence(p, own_late)
    other_late = shift(own_late, "core", 2, 1)
    p = lax.all_to_all(p, "z", 0, 0, tiled=True)
    w_out = call(out_body, struct((D, D)), [SMEM] + [VMEM] * 4, [held, held, wide], 1 << 20, 1 << 22, name="unpack_out")(
        me, own, other, own_late, other_late
    )
    p, w_out = fence(p, w_out)
    c = call(context_body, struct((NX, L, 2 * WX)), [SMEM, VMEM, ANY], flops=1 << 29, name="context")(me, p, v)
    c = lax.all_to_all(c, "x", 0, 0, tiled=True)
    return call(mixed_body, struct((2, L, D)), [SMEM, VMEM, VMEM], flops=1 << 30, name="mix")(tally, c, w_out)


def solution(mesh):
    axes = ("y", "core", "x", "z")
    grid = Mesh(mesh.devices.reshape(NY, NC, NX, NZ), axes)
    weight = P(("x", "z"), None)
    return jax.shard_map(
        per_device,
        mesh=grid,
        in_specs=(P(axes, None, None), P(), weight, weight, weight, weight, P(axes)),
        out_specs=P(axes, None, None),
        check_vma=False,
    )
```

```python
import functools
import math

import jax
import jax.numpy as jnp
from jax import lax
from jax.experimental import pallas as pl
from jax.experimental.pallas import tpu as pltpu
from jax.sharding import Mesh, PartitionSpec as P

D = 768
HEADS = 12
HD = 64
L = 256
NY, NC, NX, NZ = 4, 2, 4, 16
ND = NX * NZ
HX = HEADS // NX
WX = HX * HD
ROWS = D // ND
RY = ROWS // NY
BF = jnp.bfloat16
F32 = jnp.float32
VMEM = pl.BlockSpec(memory_space=pltpu.VMEM)
ANY = pl.BlockSpec()
HBM = pl.BlockSpec(memory_space=pltpu.HBM)
SMEM = pl.BlockSpec(memory_space=pltpu.SMEM)
VLIMIT = 24 * 1024 * 1024
VMOST = 60 * 1024 * 1024


def call(body, out, ins, scratch=(), flops=0, nbytes=1 << 20, name=None, outs=None, limit=VLIMIT):
    return pl.pallas_call(
        body,
        out_shape=out,
        in_specs=ins,
        out_specs=outs or jax.tree.map(lambda _: VMEM, out),
        scratch_shapes=list(scratch),
        compiler_params=pltpu.CompilerParams(vmem_limit_bytes=limit),
        cost_estimate=pl.CostEstimate(flops=flops, bytes_accessed=nbytes, transcendentals=0),
        name=name,
    )


def first_body(me, tally, x_hbm, g_hbm, q_hbm, k_hbm, v_hbm, o_hbm, out_ref, normed_ref, x_ref, g_ref, near, tile, sems):
    y, first = me[0] // 128, me[0] // 64 % 2 == 0
    weights = [pltpu.make_async_copy(w, near.at[i], sems.at[i]) for i, w in enumerate((q_hbm, k_hbm, v_hbm, o_hbm))]
    others = [pltpu.make_async_copy(x_hbm, x_ref, sems.at[4]), pltpu.make_async_copy(g_hbm, g_ref, sems.at[5])]
    for copy in weights + others:
        copy.start()
    for copy in weights:
        copy.wait()

    def rows(i):
        all_rows = near[i].astype(F32)
        got = all_rows[:RY]
        for j in range(1, NY):
            got = jnp.where(y == j, all_rows[j * RY : j * RY + RY], got)
        return got

    q, k, v, o = (rows(i) for i in range(4))
    o = jnp.where(first, o[:, :384], o[:, 384:])
    count = jnp.full((1, 32), tally[0].astype(F32))
    for x in range(NX):
        mine = jnp.concatenate([w[:, WX * x : WX * x + WX] for w in (q, k, v)], axis=1)
        main = jnp.where(first, mine[:, :256], mine[:, 256:512])
        rest = jnp.where(first, mine[:, 512:544], mine[:, 544:576])
        for r in range(RY):
            for c in range(2):
                tile[2 * r + c : 2 * r + c + 1, :] = main[r : r + 1, 128 * c : 128 * c + 128]
            for c in range(3):
                tile[7 + 3 * r + c : 8 + 3 * r + c, :] = o[r : r + 1, 128 * c : 128 * c + 128]
        tile[6:7, :] = jnp.concatenate([rest[r : r + 1] for r in range(RY)] + [count], axis=1)
        made = tile[...].astype(BF)
        for z in range(NZ):
            out_ref[x * NZ + z] = made
    for copy in others:
        copy.wait()
    scale = g_ref[...].reshape(1, D)
    for r in range(2):
        x = x_ref[r * L : (r + 1) * L, :].astype(F32)
        mean = jnp.sum(x, axis=-1, keepdims=True) * (1.0 / D)
        x = x - mean
        var = jnp.sum(x * x, axis=-1, keepdims=True) * (1.0 / D)
        normed = (x * lax.rsqrt(var + 1e-05) * scale).astype(BF)
        live = (r < tally[0]).astype(BF)
        normed_ref[r * L : (r + 1) * L, :] = normed * live


def split_body(pieces_ref, early_ref, late_ref, count_ref):
    early = pieces_ref[:, 0:8, :]
    for y in range(NY):
        early_ref[y] = early
    late_ref[...] = pieces_ref[:, 8:16, :].reshape(ND * 8, 128)
    count_ref[...] = jnp.sum(early[:, 6, :].astype(F32), axis=0, keepdims=True)


def take(held, core, y, s):
    return held[core, y, pl.ds(s, ND, stride=8), :]


def in_body(me, own_ref, other_ref, w_ref, held, wide):
    core = me[0] // 64 % 2
    held[core] = own_ref[...].astype(F32)
    held[1 - core] = other_ref[...].astype(F32)
    for y in range(NY):
        rest = [take(held, c, y, 6) for c in range(2)]
        for r in range(RY):
            rows = pl.ds(y * RY + r, ND, stride=ROWS)
            for k in range(4):
                wide[k, rows, :] = take(held, k // 2, y, 2 * r + k % 2)
            cut = [part[:, 32 * r : 32 * r + 32] for part in rest]
            wide[4, rows, :] = jnp.concatenate(cut + [jnp.zeros((ND, 64), F32)], axis=1)
    for k in range(5):
        w_ref[:, 128 * k : 128 * k + 128] = wide[k].astype(BF)


def out_body(me, own_a, other_a, own_b, other_b, w_ref, held_a, held_b, wide):
    y0, core = me[0] // 128, me[0] // 64 % 2
    held_a[core] = own_a[...].astype(F32)
    held_a[1 - core] = other_a[...].astype(F32)
    for g, back in enumerate((0, 1, -1, 2)):
        y = (y0 - back + NY) % NY
        held_b[core, y] = own_b[g].astype(F32)
        held_b[1 - core, y] = other_b[g].astype(F32)
    for y in range(NY):
        for r in range(RY):
            rows = pl.ds(y * RY + r, ND, stride=ROWS)
            for c in range(2):
                for k in range(3):
                    s = 7 + 3 * r + k
                    wide[3 * c + k, rows, :] = take(held_a, c, y, s) if s < 8 else take(held_b, c, y, s - 8)
    for k in range(6):
        w_ref[:, 128 * k : 128 * k + 128] = wide[k].astype(BF)


def side_by_side(array, start):
    return jnp.concatenate([array[:L, start : start + HD], array[L:, start : start + HD]], axis=1)


def logits_body(x0, x1, x2, x3, w_ref, s_ref, v_ref, q_ref, k_ref):
    for g, x_ref in enumerate((x0, x1, x2, x3)):
        made = jnp.dot(x_ref[...], w_ref[...], preferred_element_type=F32).astype(BF)
        place = slice(128 * g, 128 * g + 128)
        for h in range(HX):
            q_ref[h, :, place] = side_by_side(made, h * HD)
            k_ref[h, :, place] = side_by_side(made, WX + h * HD)
            v_ref[h, :, place] = side_by_side(made, 2 * WX + h * HD)
    for h in range(HX):
        s = lax.dot_general(q_ref[h], k_ref[h], (((1,), (1,)), ((), ())), preferred_element_type=F32)
        s_ref[:, 16 * h : 16 * h + 16, :] = s.astype(BF).reshape(NZ, 16, L)


def softmax_body(count_ref, s_ref, p_ref):
    depth = count_ref[...][:, 96:97]
    s = s_ref[0].astype(F32)
    for z in range(1, NZ):
        s = s + s_ref[z].astype(F32)
    s = s / (math.sqrt(HD) * jnp.sqrt(depth))
    e = jnp.exp(s - jnp.max(s, axis=-1, keepdims=True))
    p = (e / jnp.sum(e, axis=-1, keepdims=True)).astype(BF)
    for z in range(NZ):
        p_ref[z] = p


def context_body(me, p_ref, v_ref, c_ref):
    x = me[0] // 16 % 4
    for h in range(HX):
        p = p_ref[:, 16 * h : 16 * h + 16, :].reshape(L, L)
        made = jnp.dot(p, v_ref[h], preferred_element_type=F32).astype(BF)
        for g, back in enumerate((0, 1, -1, 2)):
            to = (x - back + NX) % NX
            c_ref[to, :, 128 * h : 128 * h + 128] = made[:, 128 * g : 128 * g + 128]


def mixed_body(tally, c_ref, w_ref, out_hbm, made_ref, sems):
    chunks = [c_ref[h // HX, :, 128 * (h % HX) : 128 * (h % HX) + 128] for h in range(HEADS)]
    copies = [pltpu.make_async_copy(made_ref.at[r], out_hbm.at[r], sems.at[r]) for r in range(2)]
    for r, copy in enumerate(copies):
        a = jnp.concatenate([chunk[:, HD * r : HD * r + HD] for chunk in chunks], axis=1)
        made = jnp.dot(a, w_ref[...], preferred_element_type=F32)
        made_ref[r] = (made * (r < tally[0]).astype(F32)).astype(BF)
        copy.start()
    for copy in copies:
        copy.wait()


def struct(shape, dtype=BF):
    return jax.ShapeDtypeStruct(shape, dtype)


def per_device(x, scale, probe, lookup, content, final, tally):
    me = lax.axis_index(("y", "core", "x", "z")).astype(jnp.int32).reshape(1)
    shift = lambda a, axis, n, d: lax.ppermute(a, axis, [(i, (i + d) % n) for i in range(n)])
    fence = lambda *a: lax.optimization_barrier(a)

    pieces, normed = call(
        first_body,
        (struct((ND, 16, 128)), struct((2 * L, D))),
        [SMEM, SMEM] + [HBM] * 6,
        [
            pltpu.VMEM((2 * L, D), BF),
            pltpu.VMEM((D,), F32),
            pltpu.VMEM((4, ROWS, D), BF),
            pltpu.VMEM((16, 128), F32),
            pltpu.SemaphoreType.DMA((6,)),
        ],
        name="first",
        outs=(ANY, ANY),
        limit=VMOST,
    )(me, tally, x.reshape(2 * L, D), scale, probe, lookup, content, final)
    pieces = lax.all_to_all(pieces, ("x", "z"), 0, 0, tiled=True)
    near, far = shift(normed, "x", NX, 1), shift(normed, "x", NX, -1)
    across = shift(near, "x", NX, 1)

    early, late, count = call(
        split_body,
        (struct((NY, ND, 8, 128)), struct((ND * 8, 128)), struct((1, 128), F32)),
        [VMEM],
        name="split",
    )(pieces)
    own = lax.all_to_all(early, "y", 0, 0, tiled=True)
    own, far, across = fence(own, far, across)
    other = shift(own, "core", 2, 1)
    own, other = own.reshape(NY, ND * 8, 128), other.reshape(NY, ND * 8, 128)
    held = pltpu.VMEM((2, NY, ND * 8, 128), F32)
    wide = pltpu.VMEM((6, D, 128), F32)
    w_in = call(in_body, struct((D, 640)), [SMEM, VMEM, VMEM], [held, wide], 1 << 20, 1 << 22, name="unpack_in")(
        me, own, other
    )
    s, v = call(
        logits_body,
        (struct((NZ, 16 * HX, L)), struct((HX, L, 8 * HD))),
        [VMEM] * 5,
        [pltpu.VMEM((HX, L, 8 * HD), BF)] * 2,
        flops=3 << 30,
        nbytes=1 << 23,
        name="logits",
    )(normed, near, far, across, w_in)

    s, late = fence(s, late)
    own_late = jnp.stack([late] + [shift(late, "y", NY, d) for d in (1, -1, 2)])
    other_late = shift(own_late, "core", 2, 1)
    w_out = call(out_body, struct((D, D)), [SMEM] + [VMEM] * 4, [held, held, wide], 1 << 20, 1 << 22, name="unpack_out")(
        me, own, other, own_late, other_late
    )
    s = lax.all_to_all(s, "z", 0, 0, tiled=True)
    s, w_out = fence(s, w_out)
    p = call(softmax_body, struct((NZ, 16 * HX, L)), [VMEM, VMEM], flops=1 << 20, name="softmax")(count, s)
    p = lax.all_to_all(p, "z", 0, 0, tiled=True)
    c = call(context_body, struct((NX, L, 2 * WX)), [SMEM, VMEM, ANY], flops=1 << 29, name="context")(me, p, v)
    c = lax.all_to_all(c, "x", 0, 0, tiled=True)
    scratch = [pltpu.VMEM((2, L, D), BF), pltpu.SemaphoreType.DMA((2,))]
    return call(mixed_body, struct((2, L, D)), [SMEM, VMEM, VMEM], scratch, 1 << 30, name="mix", outs=HBM)(tally, c, w_out)


def solution(mesh):
    axes = ("y", "core", "x", "z")
    grid = Mesh(mesh.devices.reshape(NY, NC, NX, NZ), axes)
    weight = P(("x", "z"), None)
    return jax.shard_map(
        per_device,
        mesh=grid,
        in_specs=(P(axes, None, None), P(), weight, weight, weight, weight, P(axes)),
        out_specs=P(axes, None, None),
        check_vma=False,
    )
```

```python
import functools
import math

import jax
import jax.numpy as jnp
from jax import lax
from jax.experimental import pallas as pl
from jax.experimental.pallas import tpu as pltpu
from jax.sharding import Mesh, PartitionSpec as P

D = 768
HEADS = 12
HD = 64
L = 256
NY, NC, NX, NZ = 4, 2, 4, 16
ND = NX * NZ
HX = HEADS // NX
WX = HX * HD
ROWS = D // ND
RY = ROWS // NY
BF = jnp.bfloat16
F32 = jnp.float32
VMEM = pl.BlockSpec(memory_space=pltpu.VMEM)
ANY = pl.BlockSpec()
HBM = pl.BlockSpec(memory_space=pltpu.HBM)
SMEM = pl.BlockSpec(memory_space=pltpu.SMEM)
VLIMIT = 24 * 1024 * 1024
VMOST = 60 * 1024 * 1024


def call(body, out, ins, scratch=(), flops=0, nbytes=1 << 20, name=None, outs=None, limit=VLIMIT):
    return pl.pallas_call(
        body,
        out_shape=out,
        in_specs=ins,
        out_specs=outs or jax.tree.map(lambda _: VMEM, out),
        scratch_shapes=list(scratch),
        compiler_params=pltpu.CompilerParams(vmem_limit_bytes=limit),
        cost_estimate=pl.CostEstimate(flops=flops, bytes_accessed=nbytes, transcendentals=0),
        name=name,
    )


def first_body(me, tally, x_hbm, g_hbm, q_hbm, k_hbm, v_hbm, o_hbm, out_ref, normed_ref, x_ref, g_ref, near, tile, sems):
    y, first = me[0] // 128, me[0] // 64 % 2 == 0
    weights = [pltpu.make_async_copy(w, near.at[i], sems.at[i]) for i, w in enumerate((q_hbm, k_hbm, v_hbm, o_hbm))]
    others = [pltpu.make_async_copy(x_hbm, x_ref, sems.at[4]), pltpu.make_async_copy(g_hbm, g_ref, sems.at[5])]
    for copy in weights + others:
        copy.start()
    for copy in weights:
        copy.wait()

    def rows(i):
        all_rows = near[i].astype(F32)
        got = all_rows[:RY]
        for j in range(1, NY):
            got = jnp.where(y == j, all_rows[j * RY : j * RY + RY], got)
        return got

    q, k, v, o = (rows(i) for i in range(4))
    o = jnp.where(first, o[:, :384], o[:, 384:])
    count = jnp.full((1, 32), tally[0].astype(F32))
    for x in range(NX):
        mine = jnp.concatenate([w[:, WX * x : WX * x + WX] for w in (q, k, v)], axis=1)
        main = jnp.where(first, mine[:, :256], mine[:, 256:512])
        rest = jnp.where(first, mine[:, 512:544], mine[:, 544:576])
        for r in range(RY):
            for c in range(2):
                tile[2 * r + c : 2 * r + c + 1, :] = main[r : r + 1, 128 * c : 128 * c + 128]
            for c in range(3):
                tile[7 + 3 * r + c : 8 + 3 * r + c, :] = o[r : r + 1, 128 * c : 128 * c + 128]
        tile[6:7, :] = jnp.concatenate([rest[r : r + 1] for r in range(RY)] + [count], axis=1)
        made = tile[...].astype(BF)
        for z in range(NZ):
            out_ref[x * NZ + z] = made
    for copy in others:
        copy.wait()
    scale = g_ref[...].reshape(1, D)
    for r in range(2):
        x = x_ref[r * L : (r + 1) * L, :].astype(F32)
        mean = jnp.sum(x, axis=-1, keepdims=True) * (1.0 / D)
        x = x - mean
        var = jnp.sum(x * x, axis=-1, keepdims=True) * (1.0 / D)
        normed = (x * lax.rsqrt(var + 1e-05) * scale).astype(BF)
        live = (r < tally[0]).astype(BF)
        normed_ref[r * L : (r + 1) * L, :] = normed * live


def split_body(pieces_ref, early_ref, late_ref, count_ref):
    early = pieces_ref[:, 0:8, :]
    for y in range(NY):
        early_ref[y] = early
    late_ref[...] = pieces_ref[:, 8:16, :].reshape(ND * 8, 128)
    count_ref[...] = jnp.sum(early[:, 6, :].astype(F32), axis=0, keepdims=True)


def take(held, core, y, s):
    return held[core, y, pl.ds(s, ND, stride=8), :]


def in_body(me, own_ref, other_ref, w_ref, held, wide):
    core = me[0] // 64 % 2
    held[core] = own_ref[...].astype(F32)
    held[1 - core] = other_ref[...].astype(F32)
    for y in range(NY):
        rest = [take(held, c, y, 6) for c in range(2)]
        for r in range(RY):
            rows = pl.ds(y * RY + r, ND, stride=ROWS)
            for k in range(4):
                wide[k, rows, :] = take(held, k // 2, y, 2 * r + k % 2)
            cut = [part[:, 32 * r : 32 * r + 32] for part in rest]
            wide[4, rows, :] = jnp.concatenate(cut + [jnp.zeros((ND, 64), F32)], axis=1)
    for k in range(5):
        w_ref[:, 128 * k : 128 * k + 128] = wide[k].astype(BF)


def out_body(me, own_a, other_a, own_b, other_b, w_ref, held_a, held_b, wide):
    y0, core = me[0] // 128, me[0] // 64 % 2
    held_a[core] = own_a[...].astype(F32)
    held_a[1 - core] = other_a[...].astype(F32)
    for g, back in enumerate((0, 1, -1, 2)):
        y = (y0 - back + NY) % NY
        held_b[core, y] = own_b[g].astype(F32)
        held_b[1 - core, y] = other_b[g].astype(F32)
    for y in range(NY):
        for r in range(RY):
            rows = pl.ds(y * RY + r, ND, stride=ROWS)
            for c in range(2):
                for k in range(3):
                    s = 7 + 3 * r + k
                    wide[3 * c + k, rows, :] = take(held_a, c, y, s) if s < 8 else take(held_b, c, y, s - 8)
    for k in range(6):
        w_ref[:, 128 * k : 128 * k + 128] = wide[k].astype(BF)


def side_by_side(array, start):
    return jnp.concatenate([array[:L, start : start + HD], array[L:, start : start + HD]], axis=1)


def logits_body(x0, x1, x2, x3, w_ref, s_ref, v_ref, q_ref, k_ref):
    for g, x_ref in enumerate((x0, x1, x2, x3)):
        made = jnp.dot(x_ref[...], w_ref[...], preferred_element_type=F32).astype(BF)
        place = slice(128 * g, 128 * g + 128)
        for h in range(HX):
            q_ref[h, :, place] = side_by_side(made, h * HD)
            k_ref[h, :, place] = side_by_side(made, WX + h * HD)
            v_ref[h, :, place] = side_by_side(made, 2 * WX + h * HD)
    for h in range(HX):
        s = lax.dot_general(q_ref[h], k_ref[h], (((1,), (1,)), ((), ())), preferred_element_type=F32)
        s_ref[:, 16 * h : 16 * h + 16, :] = s.astype(BF).reshape(NZ, 16, L)


def softmax_body(count_ref, s_ref, p_ref):
    depth = count_ref[...][:, 96:97]
    s = s_ref[0].astype(F32)
    for z in range(1, NZ):
        s = s + s_ref[z].astype(F32)
    s = s / (math.sqrt(HD) * jnp.sqrt(depth))
    e = jnp.exp(s - jnp.max(s, axis=-1, keepdims=True))
    p = (e / jnp.sum(e, axis=-1, keepdims=True)).astype(BF)
    for z in range(NZ):
        p_ref[z] = p


def context_body(me, p_ref, v_ref, c_ref):
    x = me[0] // 16 % 4
    for h in range(HX):
        p = p_ref[:, 16 * h : 16 * h + 16, :].reshape(L, L)
        made = jnp.dot(p, v_ref[h], preferred_element_type=F32).astype(BF)
        for g, back in enumerate((0, 1, -1, 2)):
            to = (x - back + NX) % NX
            c_ref[to, :, 128 * h : 128 * h + 128] = made[:, 128 * g : 128 * g + 128]


def mixed_body(tally, c_ref, w_ref, out_hbm, made_ref, sems):
    chunks = [c_ref[h // HX, :, 128 * (h % HX) : 128 * (h % HX) + 128] for h in range(HEADS)]
    copies = [pltpu.make_async_copy(made_ref.at[r], out_hbm.at[r], sems.at[r]) for r in range(2)]
    for r, copy in enumerate(copies):
        a = jnp.concatenate([chunk[:, HD * r : HD * r + HD] for chunk in chunks], axis=1)
        made = jnp.dot(a, w_ref[...], preferred_element_type=F32)
        made_ref[r] = (made * (r < tally[0]).astype(F32)).astype(BF)
        copy.start()
    for copy in copies:
        copy.wait()


def struct(shape, dtype=BF):
    return jax.ShapeDtypeStruct(shape, dtype)


def per_device(x, scale, probe, lookup, content, final, tally):
    me = lax.axis_index(("y", "core", "x", "z")).astype(jnp.int32).reshape(1)
    shift = lambda a, axis, n, d: lax.ppermute(a, axis, [(i, (i + d) % n) for i in range(n)])
    fence = lambda *a: lax.optimization_barrier(a)

    pieces, normed = call(
        first_body,
        (struct((ND, 16, 128)), struct((2 * L, D))),
        [SMEM, SMEM] + [HBM] * 6,
        [
            pltpu.VMEM((2 * L, D), BF),
            pltpu.VMEM((D,), F32),
            pltpu.VMEM((4, ROWS, D), BF),
            pltpu.VMEM((16, 128), F32),
            pltpu.SemaphoreType.DMA((6,)),
        ],
        name="first",
        outs=(ANY, ANY),
        limit=VMOST,
    )(me, tally, x.reshape(2 * L, D), scale, probe, lookup, content, final)
    pieces = lax.all_to_all(pieces, ("x", "z"), 0, 0, tiled=True)
    near, far = shift(normed, "x", NX, 1), shift(normed, "x", NX, -1)
    across = shift(near, "x", NX, 1)

    early, late, count = call(
        split_body,
        (struct((NY, ND, 8, 128)), struct((ND * 8, 128)), struct((1, 128), F32)),
        [VMEM],
        name="split",
    )(pieces)
    own = lax.all_to_all(early, "y", 0, 0, tiled=True)
    own, far, across = fence(own, far, across)
    other = shift(own, "core", 2, 1)
    own, other = own.reshape(NY, ND * 8, 128), other.reshape(NY, ND * 8, 128)
    held = pltpu.VMEM((2, NY, ND * 8, 128), F32)
    wide = pltpu.VMEM((6, D, 128), F32)
    w_in = call(in_body, struct((D, 640)), [SMEM, VMEM, VMEM], [held, wide], 1 << 20, 1 << 22, name="unpack_in")(
        me, own, other
    )
    s, v = call(
        logits_body,
        (struct((NZ, 16 * HX, L)), struct((HX, L, 8 * HD))),
        [VMEM] * 5,
        [pltpu.VMEM((HX, L, 8 * HD), BF)] * 2,
        flops=3 << 30,
        nbytes=1 << 23,
        name="logits",
    )(normed, near, far, across, w_in)

    s = lax.all_to_all(s, "z", 0, 0, tiled=True)
    p = call(softmax_body, struct((NZ, 16 * HX, L)), [VMEM, VMEM], flops=1 << 20, name="softmax")(count, s)
    p, late = fence(p, late)
    own_late = jnp.stack([late] + [shift(late, "y", NY, d) for d in (1, -1, 2)])
    other_late = shift(own_late, "core", 2, 1)
    w_out = call(out_body, struct((D, D)), [SMEM] + [VMEM] * 4, [held, held, wide], 1 << 20, 1 << 22, name="unpack_out")(
        me, own, other, own_late, other_late
    )
    p = lax.all_to_all(p, "z", 0, 0, tiled=True)
    p, w_out = fence(p, w_out)
    c = call(context_body, struct((NX, L, 2 * WX)), [SMEM, VMEM, ANY], flops=1 << 29, name="context")(me, p, v)
    c = lax.all_to_all(c, "x", 0, 0, tiled=True)
    scratch = [pltpu.VMEM((2, L, D), BF), pltpu.SemaphoreType.DMA((2,))]
    return call(mixed_body, struct((2, L, D)), [SMEM, VMEM, VMEM], scratch, 1 << 30, name="mix", outs=HBM)(tally, c, w_out)


def solution(mesh):
    axes = ("y", "core", "x", "z")
    grid = Mesh(mesh.devices.reshape(NY, NC, NX, NZ), axes)
    weight = P(("x", "z"), None)
    return jax.shard_map(
        per_device,
        mesh=grid,
        in_specs=(P(axes, None, None), P(), weight, weight, weight, weight, P(axes)),
        out_specs=P(axes, None, None),
        check_vma=False,
    )
```

```python
import functools
import math

import jax
import jax.numpy as jnp
from jax import lax
from jax.experimental import pallas as pl
from jax.experimental.pallas import tpu as pltpu
from jax.sharding import Mesh, PartitionSpec as P

D = 768
HEADS = 12
HD = 64
L = 256
NY, NC, NX, NZ = 4, 2, 4, 16
ND = NX * NZ
HX = HEADS // NX
WX = HX * HD
ROWS = D // ND
RY = ROWS // NY
BF = jnp.bfloat16
F32 = jnp.float32
VMEM = pl.BlockSpec(memory_space=pltpu.VMEM)
ANY = pl.BlockSpec()
HBM = pl.BlockSpec(memory_space=pltpu.HBM)
SMEM = pl.BlockSpec(memory_space=pltpu.SMEM)
VLIMIT = 24 * 1024 * 1024
VMOST = 60 * 1024 * 1024
VROOM = 45000000


def call(body, out, ins, scratch=(), flops=0, nbytes=1 << 20, name=None, outs=None, limit=VLIMIT):
    return pl.pallas_call(
        body,
        out_shape=out,
        in_specs=ins,
        out_specs=outs or jax.tree.map(lambda _: VMEM, out),
        scratch_shapes=list(scratch),
        compiler_params=pltpu.CompilerParams(vmem_limit_bytes=limit),
        cost_estimate=pl.CostEstimate(flops=flops, bytes_accessed=nbytes, transcendentals=0),
        name=name,
    )


def first_body(me, tally, x_hbm, g_hbm, q_hbm, k_hbm, v_hbm, o_hbm, out_ref, normed_ref, x_ref, g_ref, near, tile, sems):
    y, first = me[0] // 128, me[0] // 64 % 2 == 0
    weights = [pltpu.make_async_copy(w, near.at[i], sems.at[i]) for i, w in enumerate((q_hbm, k_hbm, v_hbm, o_hbm))]
    others = [pltpu.make_async_copy(x_hbm, x_ref, sems.at[4]), pltpu.make_async_copy(g_hbm, g_ref, sems.at[5])]
    for copy in weights + others:
        copy.start()
    for copy in weights:
        copy.wait()

    def rows(i):
        all_rows = near[i].astype(F32)
        got = all_rows[:RY]
        for j in range(1, NY):
            got = jnp.where(y == j, all_rows[j * RY : j * RY + RY], got)
        return got

    q, k, v, o = (rows(i) for i in range(4))
    o = jnp.where(first, o[:, :384], o[:, 384:])
    count = jnp.full((1, 32), tally[0].astype(F32))
    for x in range(NX):
        mine = jnp.concatenate([w[:, WX * x : WX * x + WX] for w in (q, k, v)], axis=1)
        main = jnp.where(first, mine[:, :256], mine[:, 256:512])
        rest = jnp.where(first, mine[:, 512:544], mine[:, 544:576])
        for r in range(RY):
            for c in range(2):
                tile[2 * r + c : 2 * r + c + 1, :] = main[r : r + 1, 128 * c : 128 * c + 128]
            for c in range(3):
                tile[7 + 3 * r + c : 8 + 3 * r + c, :] = o[r : r + 1, 128 * c : 128 * c + 128]
        tile[6:7, :] = jnp.concatenate([rest[r : r + 1] for r in range(RY)] + [count], axis=1)
        made = tile[...].astype(BF)
        for z in range(NZ):
            out_ref[x * NZ + z] = made
    for copy in others:
        copy.wait()
    scale = g_ref[...].reshape(1, D)
    for r in range(2):
        x = x_ref[r * L : (r + 1) * L, :].astype(F32)
        mean = jnp.sum(x, axis=-1, keepdims=True) * (1.0 / D)
        x = x - mean
        var = jnp.sum(x * x, axis=-1, keepdims=True) * (1.0 / D)
        normed = (x * lax.rsqrt(var + 1e-05) * scale).astype(BF)
        live = (r < tally[0]).astype(BF)
        normed_ref[r * L : (r + 1) * L, :] = normed * live


def split_body(pieces_ref, early_ref, late_ref, count_ref):
    early = pieces_ref[:, 0:8, :]
    for y in range(NY):
        early_ref[y] = early
    late_ref[...] = pieces_ref[:, 8:16, :].reshape(ND * 8, 128)
    count_ref[...] = jnp.sum(early[:, 6, :].astype(F32), axis=0, keepdims=True)


def take(held, core, y, s):
    return held[core, y, pl.ds(s, ND, stride=8), :]


def in_body(me, own_ref, other_ref, w_ref, held, wide):
    core = me[0] // 64 % 2
    held[core] = own_ref[...].astype(F32)
    held[1 - core] = other_ref[...].astype(F32)
    for y in range(NY):
        rest = [take(held, c, y, 6) for c in range(2)]
        for r in range(RY):
            rows = pl.ds(y * RY + r, ND, stride=ROWS)
            for k in range(4):
                wide[k, rows, :] = take(held, k // 2, y, 2 * r + k % 2)
            cut = [part[:, 32 * r : 32 * r + 32] for part in rest]
            wide[4, rows, :] = jnp.concatenate(cut + [jnp.zeros((ND, 64), F32)], axis=1)
    for k in range(5):
        w_ref[:, 128 * k : 128 * k + 128] = wide[k].astype(BF)


def out_body(me, own_a, other_a, own_b, other_b, w_ref, held_a, held_b, wide):
    y0, core = me[0] // 128, me[0] // 64 % 2
    held_a[core] = own_a[...].astype(F32)
    held_a[1 - core] = other_a[...].astype(F32)
    for g, back in enumerate((0, 1, -1, 2)):
        y = (y0 - back + NY) % NY
        held_b[core, y] = own_b[g].astype(F32)
        held_b[1 - core, y] = other_b[g].astype(F32)
    for y in range(NY):
        for r in range(RY):
            rows = pl.ds(y * RY + r, ND, stride=ROWS)
            for c in range(2):
                for k in range(3):
                    s = 7 + 3 * r + k
                    wide[3 * c + k, rows, :] = take(held_a, c, y, s) if s < 8 else take(held_b, c, y, s - 8)
    for k in range(6):
        w_ref[:, 128 * k : 128 * k + 128] = wide[k].astype(BF)


def side_by_side(array, start):
    return jnp.concatenate([array[:L, start : start + HD], array[L:, start : start + HD]], axis=1)


def logits_body(x0, x1, x2, x3, w_ref, s_ref, v_ref, q_ref, k_ref):
    for g, x_ref in enumerate((x0, x1, x2, x3)):
        made = jnp.dot(x_ref[...], w_ref[...], preferred_element_type=F32).astype(BF)
        place = slice(128 * g, 128 * g + 128)
        for h in range(HX):
            q_ref[h, :, place] = side_by_side(made, h * HD)
            k_ref[h, :, place] = side_by_side(made, WX + h * HD)
            v_ref[h, :, place] = side_by_side(made, 2 * WX + h * HD)
    for h in range(HX):
        s = lax.dot_general(q_ref[h], k_ref[h], (((1,), (1,)), ((), ())), preferred_element_type=F32)
        s_ref[:, 16 * h : 16 * h + 16, :] = s.astype(BF).reshape(NZ, 16, L)


def softmax_body(count_ref, s_ref, p_ref):
    depth = count_ref[...][:, 96:97]
    s = s_ref[0].astype(F32)
    for z in range(1, NZ):
        s = s + s_ref[z].astype(F32)
    s = s / (math.sqrt(HD) * jnp.sqrt(depth))
    e = jnp.exp(s - jnp.max(s, axis=-1, keepdims=True))
    p = (e / jnp.sum(e, axis=-1, keepdims=True)).astype(BF)
    for z in range(NZ):
        p_ref[z] = p


def context_body(me, p_ref, v_ref, c_ref):
    x = me[0] // 16 % 4
    for h in range(HX):
        p = p_ref[:, 16 * h : 16 * h + 16, :].reshape(L, L)
        made = jnp.dot(p, v_ref[h], preferred_element_type=F32).astype(BF)
        for g, back in enumerate((0, 1, -1, 2)):
            to = (x - back + NX) % NX
            c_ref[to, :, 128 * h : 128 * h + 128] = made[:, 128 * g : 128 * g + 128]


def mixed_body(tally, c_ref, w_ref, out_hbm, made_ref, sems):
    chunks = [c_ref[h // HX, :, 128 * (h % HX) : 128 * (h % HX) + 128] for h in range(HEADS)]
    copies = [pltpu.make_async_copy(made_ref.at[r], out_hbm.at[r], sems.at[r]) for r in range(2)]
    for r, copy in enumerate(copies):
        a = jnp.concatenate([chunk[:, HD * r : HD * r + HD] for chunk in chunks], axis=1)
        made = jnp.dot(a, w_ref[...], preferred_element_type=F32)
        made_ref[r] = (made * (r < tally[0]).astype(F32)).astype(BF)
        copy.start()
    for copy in copies:
        copy.wait()


def struct(shape, dtype=BF):
    return jax.ShapeDtypeStruct(shape, dtype)


def per_device(x, scale, probe, lookup, content, final, tally):
    me = lax.axis_index(("y", "core", "x", "z")).astype(jnp.int32).reshape(1)
    shift = lambda a, axis, n, d: lax.ppermute(a, axis, [(i, (i + d) % n) for i in range(n)])
    fence = lambda *a: lax.optimization_barrier(a)

    pieces, normed = call(
        first_body,
        (struct((ND, 16, 128)), struct((2 * L, D))),
        [SMEM, SMEM] + [HBM] * 6,
        [
            pltpu.VMEM((2 * L, D), BF),
            pltpu.VMEM((D,), F32),
            pltpu.VMEM((4, ROWS, D), BF),
            pltpu.VMEM((16, 128), F32),
            pltpu.SemaphoreType.DMA((6,)),
        ],
        name="first",
        outs=(ANY, ANY),
        limit=VMOST,
    )(me, tally, x.reshape(2 * L, D), scale, probe, lookup, content, final)
    pieces = lax.all_to_all(pieces, ("x", "z"), 0, 0, tiled=True)
    near, far = shift(normed, "x", NX, 1), shift(normed, "x", NX, -1)
    across = shift(near, "x", NX, 1)

    early, late, count = call(
        split_body,
        (struct((NY, ND, 8, 128)), struct((ND * 8, 128)), struct((1, 128), F32)),
        [VMEM],
        name="split",
    )(pieces)
    own = lax.all_to_all(early, "y", 0, 0, tiled=True)
    own, far, across = fence(own, far, across)
    other = shift(own, "core", 2, 1)
    own, other = own.reshape(NY, ND * 8, 128), other.reshape(NY, ND * 8, 128)
    held = pltpu.VMEM((2, NY, ND * 8, 128), F32)
    wide = pltpu.VMEM((6, D, 128), F32)
    w_in = call(in_body, struct((D, 640)), [SMEM, VMEM, VMEM], [held, wide], 1 << 20, 1 << 22, name="unpack_in")(
        me, own, other
    )
    s, v = call(
        logits_body,
        (struct((NZ, 16 * HX, L)), struct((HX, L, 8 * HD))),
        [VMEM] * 5,
        [pltpu.VMEM((HX, L, 8 * HD), BF)] * 2,
        flops=3 << 30,
        nbytes=1 << 23,
        name="logits",
        outs=(VMEM, ANY),
        limit=VROOM,
    )(normed, near, far, across, w_in)

    s = lax.all_to_all(s, "z", 0, 0, tiled=True)
    p = call(softmax_body, struct((NZ, 16 * HX, L)), [VMEM, VMEM], flops=1 << 20, name="softmax")(count, s)
    p, late = fence(p, late)
    own_late = jnp.stack([late] + [shift(late, "y", NY, d) for d in (1, -1, 2)])
    other_late = shift(own_late, "core", 2, 1)
    w_out = call(out_body, struct((D, D)), [SMEM] + [VMEM] * 4, [held, held, wide], 1 << 20, 1 << 22, name="unpack_out")(
        me, own, other, own_late, other_late
    )
    p = lax.all_to_all(p, "z", 0, 0, tiled=True)
    p, w_out = fence(p, w_out)
    c = call(context_body, struct((NX, L, 2 * WX)), [SMEM, VMEM, ANY], flops=1 << 29, name="context")(me, p, v)
    c = lax.all_to_all(c, "x", 0, 0, tiled=True)
    scratch = [pltpu.VMEM((2, L, D), BF), pltpu.SemaphoreType.DMA((2,))]
    return call(mixed_body, struct((2, L, D)), [SMEM, VMEM, VMEM], scratch, 1 << 30, name="mix", outs=HBM)(tally, c, w_out)


def solution(mesh):
    axes = ("y", "core", "x", "z")
    grid = Mesh(mesh.devices.reshape(NY, NC, NX, NZ), axes)
    weight = P(("x", "z"), None)
    return jax.shard_map(
        per_device,
        mesh=grid,
        in_specs=(P(axes, None, None), P(), weight, weight, weight, weight, P(axes)),
        out_specs=P(axes, None, None),
        check_vma=False,
    )
```
